512 devices in a mesh: gx: 8 (over z), gy: 8 (over x, y_hi), gz: 8 (over y_lo, core).
Axes of the slice: x: 4, y: 8 (y_hi: 2, y_lo: 4; y = y_hi * 4 + y_lo), z: 8, core: 2. Of those that a mesh axis runs over, the one named last changes fastest.
Arguments:
- inputs: bfloat16 [2048, 6144], P(('gx', 'gy'), 'gz'), may hold values from -6 to 6
- value_weight: bfloat16 [6144, 6144], P(('gz', 'gx'), 'gy'), may hold values from -0.078125 to 0.078125
- probs: bfloat16 [48, 2048, 2048], P('gy', 'gz', 'gx'), may hold values from 0 to 1, as said below
- attended: bfloat16 [2048, 6144], P(('gz', 'gx'), 'gy'), may hold values from -6 to 6
- out_weight: bfloat16 [6144, 6144], P(('gy', 'gz'), 'gx'), may hold values from -0.078125 to 0.078125
- out_grad: bfloat16 [2048, 6144], P(('gz', 'gy'), 'gx'), may hold values from -6 to 6
Outputs:
- grad_inputs: bfloat16 [2048, 6144], P(('gx', 'gy'), 'gz')
- grad_value_weight: float32 [6144, 6144], P(('gz', 'gx'), 'gy')
- grad_out_weight: float32 [6144, 6144], P(('gy', 'gz'), 'gx')
The draws below stay inside these ranges and needn't reach their ends.
Inputs may be any that keep to these rules, and one draw needn't show every extreme that they name: probs[h, q, k] is zero where k > q, and each row sums to one up to rounding.
All inputs are finite; a program needn't handle non-finite values.
Results may differ from the reference program's by a relative error of at most 0.03.
Values may be sent and summed in bfloat16 or wider, within the bound.
No kernel may reach another device: no remote copies, remote signals or barrier semaphores. Data moves between devices by JAX's collectives and lax.ppermute only.
A program may use at most 64 MiB of HBM per device.

```python
import math
import jax
import jax.numpy as jnp
from jax import lax

D = 6144
HEADS = 48
HEAD_DIM = 128
HW = 6144
TOKENS = 2048
N_GX = 8
N_GY = 8
N_GZ = 8


def draw_probs(key, part):
    key = jax.random.fold_in(key, 11)
    positions = jnp.arange(TOKENS)
    causal = positions[None, :] <= positions[:, None]

    def one_head(index):
        head_key = jax.random.fold_in(key, index)
        logits = 2.0 * jax.random.normal(head_key, (TOKENS, TOKENS), jnp.float32)
        logits = jnp.where(causal, logits, -1e+30)
        return jax.nn.softmax(logits, axis=-1).astype(jnp.bfloat16)
    return lax.map(one_head, jnp.arange(HEADS))


def shard_levels(own_key, dims, shards, smallest, top_value):
    level = 1.0
    for dim, blocks in shards:
        steps = jax.random.uniform(jax.random.fold_in(jax.random.fold_in(own_key, 6), dim), (blocks,), jnp.float32, smallest / len(shards), top_value / len(shards))
        level = level * jnp.repeat(jnp.exp(steps), dims[dim] // blocks).reshape((-1,) + (1,) * (len(dims) - 1 - dim))
    return level


def noise(stream_key, shape, scale, bound, cuts=(), kind=jnp.bfloat16):
    array = jax.random.normal(stream_key, shape, jnp.float32) * scale
    if len(cuts) > 0:
        array = shard_levels(stream_key, shape, cuts, -0.22, 0.18) * array
    return jnp.clip(array, min=-bound, max=bound).astype(kind)


def setup_inputs(seed: int = 0) -> dict:
    splits = jax.random.split(jax.random.key(seed), 7)
    return {
        "inputs": noise(splits[0], (TOKENS, D), 1.0, 6.0, ((0, 64), (1, 8))),
        "value_weight": noise(splits[1], (D, HW), D ** -0.5, 0.078125, ((0, 64), (1, 8))),
        "probs": draw_probs(jax.random.fold_in(splits[6], 71), 0),
        "attended": noise(splits[3], (TOKENS, HW), 1.0, 6.0, ((0, 64), (1, 8))),
        "out_weight": noise(splits[4], (HW, D), HW ** -0.5, 0.078125, ((0, 64), (1, 8))),
        "out_grad": noise(splits[5], (TOKENS, D), 1.0, 6.0, ((0, 64), (1, 8))),
    }


def block_sum(left, right, blocks, grad_scale):
    block_rows = left.shape[0] // blocks
    left_blocks = left.reshape(blocks, block_rows, left.shape[1])
    right_blocks = right.reshape(blocks, block_rows, right.shape[1])

    def add_block(running, operands):
        partial_term = lax.dot_general(operands[0], operands[1], (((0,), (0,)), ((), ())), preferred_element_type=jnp.float32) * grad_scale
        rounded = lax.optimization_barrier(partial_term.astype(jnp.bfloat16))
        return (running + rounded.astype(jnp.float32), None)
    initial = jnp.zeros((left.shape[1], right.shape[1]), jnp.float32)
    return lax.scan(add_block, initial, (left_blocks, right_blocks))[0]

def reference(inputs, value_weight, probs, attended, out_weight, out_grad):
    grad_scale = 1.0 / math.sqrt(TOKENS)
    head_grad = jnp.dot(out_grad, out_weight.T, preferred_element_type=jnp.float32).astype(jnp.bfloat16)
    grad_heads = head_grad.reshape(TOKENS, HEADS, HEAD_DIM).transpose(1, 0, 2)

    def per_head(operands):
        return jnp.dot(operands[0].T, operands[1], preferred_element_type=jnp.float32).astype(jnp.bfloat16)
    value_heads = lax.map(per_head, (probs, grad_heads))
    value_grad = value_heads.transpose(1, 0, 2).reshape(TOKENS, HW)
    grad_out_weight = block_sum(attended, out_grad, N_GZ, grad_scale)
    grad_value_weight = block_sum(inputs, value_grad, N_GX, grad_scale)
    column_block = HW // N_GY
    grad_split = value_grad.reshape(TOKENS, N_GY, column_block).transpose(1, 0, 2)
    weight_split = value_weight.reshape(D, N_GY, column_block).transpose(1, 0, 2)

    def add_columns(running, operands):
        partial_term = jnp.dot(operands[0], operands[1].T, preferred_element_type=jnp.float32)
        rounded = lax.optimization_barrier(partial_term.astype(jnp.bfloat16))
        return (running + rounded.astype(jnp.float32), None)
    initial = jnp.zeros((TOKENS, D), jnp.float32)
    grad_inputs = lax.scan(add_columns, initial, (grad_split, weight_split))[0].astype(jnp.bfloat16)
    return (grad_inputs, grad_value_weight, grad_out_weight)
```

```python
import math

import jax
import jax.numpy as jnp
from jax import lax
from jax.sharding import PartitionSpec as P

HEAD_DIM = 128
Y_GROUPS = [[0, 2, 4, 6], [1, 3, 5, 7]]
CORE_GROUPS = [[0, 1], [2, 3], [4, 5], [6, 7]]
F32 = jnp.float32
BF16 = jnp.bfloat16


def spread(x, axis, groups=None):
    n = len(groups[0]) if groups else lax.axis_size(axis)
    copies = jnp.broadcast_to(x[None], (n,) + x.shape)
    return lax.all_to_all(copies, axis, 0, 0, tiled=True, axis_index_groups=groups)


def scatter_sum(x, axis):
    n = lax.axis_size(axis)
    parts = x.reshape((n, x.shape[0] // n) + x.shape[1:])
    parts = lax.all_to_all(parts, axis, 0, 0, tiled=True)
    return jnp.sum(parts.astype(F32), axis=0)


def dot(a, b, dims):
    return lax.dot_general(a, b, (dims, ((), ())), preferred_element_type=F32)


def body(inputs, value_weight, probs, attended, out_weight, out_grad):
    tokens_all = probs.shape[1] * lax.axis_size("gz")
    grad_scale = 1.0 / math.sqrt(tokens_all)
    heads = probs.shape[0]
    width = heads * HEAD_DIM
    rows = inputs.shape[0]
    depth = value_weight.shape[0]

    side = lax.all_gather(jnp.concatenate([value_weight, attended]), "gx", axis=0)
    weight_all = side[:, :depth].reshape(-1, width)
    saved = side[:, depth:].reshape(-1, width)

    quarter = lax.all_gather(out_weight, "gz", axis=0, axis_index_groups=Y_GROUPS)
    halves = spread(quarter, "gz", CORE_GROUPS)
    out_all = halves.transpose(1, 0, 2, 3).reshape(width, -1)
    both = spread(jnp.concatenate([out_grad, inputs]), "gy")
    grad_all = both[:, :rows].reshape(-1, out_grad.shape[1])
    input_all = both[:, rows:].reshape(-1, inputs.shape[1])

    head_partial = dot(grad_all, out_all, ((1,), (1,))).astype(BF16)
    head_rows = scatter_sum(head_partial, "gx").astype(BF16)
    head_grad = spread(head_rows, "gx").reshape(-1, heads, HEAD_DIM)

    out_terms = (dot(saved, grad_all, ((0,), (0,))) * grad_scale).astype(BF16)
    grad_out_weight = lax.psum_scatter(out_terms, "gz", scatter_dimension=0, tiled=True)

    value_partial = jnp.einsum("hqk,qhd->khd", probs, head_grad, preferred_element_type=F32)
    value_partial = value_partial.reshape(-1, width).astype(BF16)
    value_rows = scatter_sum(value_partial, "gz").astype(BF16)
    value_grad = lax.all_gather(value_rows, "gz", axis=0, tiled=True)

    value_terms = (dot(input_all, value_grad, ((0,), (0,))) * grad_scale).astype(BF16)
    grad_value_weight = lax.psum_scatter(value_terms, "gx", scatter_dimension=0, tiled=True)
    input_partial = dot(value_grad, weight_all, ((1,), (1,))).astype(BF16)
    grad_inputs = scatter_sum(input_partial, "gy").astype(BF16)
    return grad_inputs, grad_value_weight.astype(F32), grad_out_weight.astype(F32)


def solution(mesh):
    in_specs = (
        P(("gx", "gy"), "gz"),
        P(("gz", "gx"), "gy"),
        P("gy", "gz", "gx"),
        P(("gz", "gx"), "gy"),
        P(("gy", "gz"), "gx"),
        P(("gz", "gy"), "gx"),
    )
    out_specs = (P(("gx", "gy"), "gz"), P(("gz", "gx"), "gy"), P(("gy", "gz"), "gx"))
    return jax.shard_map(body, mesh=mesh, in_specs=in_specs, out_specs=out_specs, check_vma=False)
```

```python
import math

import jax
import jax.numpy as jnp
from jax import lax
from jax.sharding import PartitionSpec as P

HEAD_DIM = 128
Y_GROUPS = [[0, 2, 4, 6], [1, 3, 5, 7]]
X_GROUPS = [[0, 2, 4, 6], [1, 3, 5, 7]]
FAR_PAIRS = [(i, i ^ 1) for i in range(8)]
F32 = jnp.float32
BF16 = jnp.bfloat16


def spread(x, axis, groups=None):
    n = len(groups[0]) if groups else lax.axis_size(axis)
    copies = jnp.broadcast_to(x[None], (n,) + x.shape)
    return lax.all_to_all(copies, axis, 0, 0, tiled=True, axis_index_groups=groups)


def exchange(x, axis):
    n = lax.axis_size(axis)
    parts = x.reshape((n, x.shape[0] // n) + x.shape[1:])
    return lax.all_to_all(parts, axis, 0, 0, tiled=True)


def scatter_sum(x, axis):
    return jnp.sum(exchange(x, axis).astype(F32), axis=0)


def scatter_sum_gy(x):
    me = lax.axis_index("gy")
    ring, far = me >> 1, me & 1
    parts = x.reshape((4, 2, x.shape[0] // 8) + x.shape[1:])
    total = lax.dynamic_index_in_dim(parts, ring, 0, False).astype(F32)
    for k in (1, 2, 3):
        pairs = [(i, (i + 2 * k) % 8) for i in range(8)]
        sent = lax.dynamic_index_in_dim(parts, (ring + k) & 3, 0, False)
        total = total + lax.ppermute(sent, "gy", pairs).astype(F32)
    sent = lax.dynamic_index_in_dim(total, 1 - far, 0, False).astype(BF16)
    kept = lax.dynamic_index_in_dim(total, far, 0, False)
    return kept + lax.ppermute(sent, "gy", FAR_PAIRS).astype(F32)

def far_pair(x):
    other = lax.ppermute(x, "gy", FAR_PAIRS)
    first = (lax.axis_index("gy") & 1) == 0
    return jnp.where(first, jnp.stack([x, other]), jnp.stack([other, x]))


def from_ring(x, k):
    return lax.ppermute(x, "gy", [(i, (i + 2 * k) % 8) for i in range(8)])


def in_ring_order(blocks):
    ring = lax.axis_index("gy") >> 1
    ordered = [lax.select_n((ring - j) & 3, *blocks) for j in range(4)]
    return jnp.stack(ordered).reshape((-1,) + blocks[0].shape[2:])


def dot(a, b, dims):
    return lax.dot_general(a, b, (dims, ((), ())), preferred_element_type=F32)


def body(inputs, value_weight, probs, attended, out_weight, out_grad):
    tokens_all = probs.shape[1] * lax.axis_size("gz")
    grad_scale = 1.0 / math.sqrt(tokens_all)
    heads = probs.shape[0]
    width = heads * HEAD_DIM
    rows = inputs.shape[0]
    depth = value_weight.shape[0]

    side = lax.all_gather(jnp.concatenate([value_weight, attended]), "gx", axis=0)
    weight_all = side[:, :depth].reshape(-1, width)
    saved = side[:, depth:].reshape(-1, width)

    pair = far_pair(out_grad)
    quarter = lax.all_gather(out_weight, "gz", axis=0, axis_index_groups=Y_GROUPS)
    pair, quarter = lax.optimization_barrier((pair, quarter))
    grad_all = spread(pair, "gy", X_GROUPS).reshape(-1, out_grad.shape[1])
    quarter = quarter.reshape((-1,) + out_weight.shape)
    sibling = lax.ppermute(quarter, "gz", FAR_PAIRS)
    first = (lax.axis_index("gz") & 1) == 0
    halves = jnp.where(
        first, jnp.stack([quarter, sibling], 1), jnp.stack([sibling, quarter], 1)
    )
    out_all = halves.reshape(width, -1)

    head_partial = dot(grad_all, out_all, ((1,), (1,))).astype(BF16)
    head_partial, late = lax.optimization_barrier((head_partial, inputs))
    head_parts = exchange(head_partial, "gx")
    out_terms = (dot(saved, grad_all, ((0,), (0,))) * grad_scale).astype(BF16)
    pair = far_pair(late)
    head_parts, out_terms, pair = lax.optimization_barrier((head_parts, out_terms, pair))
    grad_out_weight = lax.psum_scatter(out_terms, "gz", scatter_dimension=0, tiled=True)
    head_rows = jnp.sum(head_parts.astype(F32), axis=0).astype(BF16)
    head_grad = spread(head_rows, "gx").reshape(-1, width)
    blocks = [pair, from_ring(pair, 1), None, from_ring(pair, 3)]
    head_grad, blocks[1], blocks[3], pair = lax.optimization_barrier(
        (head_grad, blocks[1], blocks[3], pair)
    )
    head_grad = head_grad.reshape(-1, heads, HEAD_DIM)

    value_partial = jnp.einsum("hqk,qhd->khd", probs, head_grad, preferred_element_type=F32)
    value_partial = value_partial.reshape(-1, width).astype(BF16)
    value_partial, pair = lax.optimization_barrier((value_partial, pair))
    value_parts = exchange(value_partial, "gz")
    blocks[2] = from_ring(pair, 2)
    value_parts, blocks[2] = lax.optimization_barrier((value_parts, blocks[2]))
    input_all = in_ring_order(blocks)
    value_rows = jnp.sum(value_parts.astype(F32), axis=0).astype(BF16)
    value_grad = lax.all_gather(value_rows, "gz", axis=0, tiled=True)

    value_terms = (dot(input_all, value_grad, ((0,), (0,))) * grad_scale).astype(BF16)
    input_partial = dot(value_grad, weight_all, ((1,), (1,))).astype(BF16)
    grad_value_weight = scatter_sum(value_terms, "gx")
    grad_inputs = scatter_sum_gy(input_partial)
    return grad_inputs.astype(BF16), grad_value_weight.astype(F32), grad_out_weight.astype(F32)


def solution(mesh):
    in_specs = (
        P(("gx", "gy"), "gz"),
        P(("gz", "gx"), "gy"),
        P("gy", "gz", "gx"),
        P(("gz", "gx"), "gy"),
        P(("gy", "gz"), "gx"),
        P(("gz", "gy"), "gx"),
    )
    out_specs = (P(("gx", "gy"), "gz"), P(("gz", "gx"), "gy"), P(("gy", "gz"), "gx"))
    return jax.shard_map(body, mesh=mesh, in_specs=in_specs, out_specs=out_specs, check_vma=False)
```

```python
import math

import jax
import jax.numpy as jnp
from jax import lax
from jax.sharding import PartitionSpec as P

HEAD_DIM = 128
Y_GROUPS = [[0, 2, 4, 6], [1, 3, 5, 7]]
CORE_GROUPS = [[0, 1], [2, 3], [4, 5], [6, 7]]
X_GROUPS = [[0, 2, 4, 6], [1, 3, 5, 7]]
FAR_PAIRS = [(i, i ^ 1) for i in range(8)]
PAD_ROWS = 128
F32 = jnp.float32
BF16 = jnp.bfloat16


def spread(x, axis, groups=None):
    n = len(groups[0]) if groups else lax.axis_size(axis)
    copies = jnp.broadcast_to(x[None], (n,) + x.shape)
    return lax.all_to_all(copies, axis, 0, 0, tiled=True, axis_index_groups=groups)


def exchange(x, axis):
    n = lax.axis_size(axis)
    parts = x.reshape((n, x.shape[0] // n) + x.shape[1:])
    return lax.all_to_all(parts, axis, 0, 0, tiled=True)


def scatter_sum(x, axis):
    return jnp.sum(exchange(x, axis).astype(F32), axis=0)


def scatter_sum_gy(x):
    me = lax.axis_index("gy")
    ring, far = me >> 1, me & 1
    parts = x.reshape((4, 2, x.shape[0] // 8) + x.shape[1:])
    total = lax.dynamic_index_in_dim(parts, ring, 0, False).astype(F32)
    for k in (1, 2, 3):
        pairs = [(i, (i + 2 * k) % 8) for i in range(8)]
        sent = lax.dynamic_index_in_dim(parts, (ring + k) & 3, 0, False)
        total = total + lax.ppermute(sent, "gy", pairs).astype(F32)
    sent = lax.dynamic_index_in_dim(total, 1 - far, 0, False).astype(BF16)
    kept = lax.dynamic_index_in_dim(total, far, 0, False)
    return kept + lax.ppermute(sent, "gy", FAR_PAIRS).astype(F32)

def far_pair(x):
    other = lax.ppermute(x, "gy", FAR_PAIRS)
    first = (lax.axis_index("gy") & 1) == 0
    return jnp.where(first, jnp.stack([x, other]), jnp.stack([other, x]))


def all_sum_gz(x, later):
    both = lax.all_gather(x, "gz", axis=0, axis_index_groups=CORE_GROUPS)
    both = both.reshape((2, 2, x.shape[0] // 2) + x.shape[1:])
    half = lax.dynamic_index_in_dim(both, lax.axis_index("gz") & 1, 1, False)
    half = jnp.sum(half.astype(F32), axis=0).astype(BF16)
    run = lax.all_gather(half, "gz", axis=0, axis_index_groups=Y_GROUPS)
    run, later = lax.optimization_barrier((run, later))
    half = jnp.sum(run.astype(F32), axis=0).astype(BF16)
    return lax.all_gather(half, "gz", axis=0, axis_index_groups=CORE_GROUPS, tiled=True), later


def dot(a, b, dims):
    return lax.dot_general(a, b, (dims, ((), ())), preferred_element_type=F32)


def body(inputs, value_weight, probs, attended, out_weight, out_grad):
    tokens_all = probs.shape[1] * lax.axis_size("gz")
    grad_scale = 1.0 / math.sqrt(tokens_all)
    heads = probs.shape[0]
    width = heads * HEAD_DIM
    depth = value_weight.shape[0]

    side = lax.all_gather(jnp.concatenate([value_weight, attended]), "gx", axis=0)
    weight_all = side[:, :depth].reshape(-1, width)
    saved = side[:, depth:].reshape(-1, width)

    pair = far_pair(out_grad)
    quarter = lax.all_gather(out_weight, "gz", axis=0, axis_index_groups=Y_GROUPS)
    pair, quarter, late = lax.optimization_barrier((pair, quarter, inputs))
    input_pair = far_pair(late)
    grad_all = spread(pair, "gy", X_GROUPS).reshape(-1, out_grad.shape[1])
    quarter = quarter.reshape((-1,) + out_weight.shape)
    sibling = lax.ppermute(quarter, "gz", FAR_PAIRS)
    first = (lax.axis_index("gz") & 1) == 0
    halves = jnp.where(
        first, jnp.stack([quarter, sibling], 1), jnp.stack([sibling, quarter], 1)
    )
    out_all = halves.reshape(width, -1)

    head_partial = dot(grad_all, out_all, ((1,), (1,))).astype(BF16)
    head_parts = exchange(head_partial, "gx")
    out_terms = (dot(saved, grad_all, ((0,), (0,))) * grad_scale).astype(BF16)
    input_pair, out_terms = lax.optimization_barrier((input_pair, out_terms))
    mine = input_pair.reshape(-1, inputs.shape[1])
    mine = jnp.pad(mine, ((0, PAD_ROWS), (0, 0)))
    head_parts, out_terms, mine = lax.optimization_barrier((head_parts, out_terms, mine))
    input_all = lax.all_gather(mine, "gy", axis=0, axis_index_groups=X_GROUPS)
    head_rows = jnp.sum(head_parts.astype(F32), axis=0).astype(BF16)
    head_grad = spread(head_rows, "gx").reshape(-1, heads, HEAD_DIM)

    value_partial = jnp.einsum("hqk,qhd->khd", probs, head_grad, preferred_element_type=F32)
    value_partial = value_partial.reshape(-1, width).astype(BF16)
    value_grad, out_terms = all_sum_gz(value_partial, out_terms)
    grad_out_weight = lax.psum_scatter(out_terms, "gz", scatter_dimension=0, tiled=True)

    input_all = input_all[:, : 2 * inputs.shape[0]].reshape(-1, inputs.shape[1])
    value_terms = (dot(input_all, value_grad, ((0,), (0,))) * grad_scale).astype(BF16)
    input_partial = dot(value_grad, weight_all, ((1,), (1,))).astype(BF16)
    grad_value_weight = scatter_sum(value_terms, "gx")
    grad_inputs = scatter_sum_gy(input_partial)
    return grad_inputs.astype(BF16), grad_value_weight.astype(F32), grad_out_weight.astype(F32)


def solution(mesh):
    in_specs = (
        P(("gx", "gy"), "gz"),
        P(("gz", "gx"), "gy"),
        P("gy", "gz", "gx"),
        P(("gz", "gx"), "gy"),
        P(("gy", "gz"), "gx"),
        P(("gz", "gy"), "gx"),
    )
    out_specs = (P(("gx", "gy"), "gz"), P(("gz", "gx"), "gy"), P(("gy", "gz"), "gx"))
    return jax.shard_map(body, mesh=mesh, in_specs=in_specs, out_specs=out_specs, check_vma=False)
```

```python
import math

import jax
import jax.numpy as jnp
from jax import lax
from jax.sharding import PartitionSpec as P

HEAD_DIM = 128
Y_GROUPS = [[0, 2, 4, 6], [1, 3, 5, 7]]
CORE_GROUPS = [[0, 1], [2, 3], [4, 5], [6, 7]]
X_GROUPS = [[0, 2, 4, 6], [1, 3, 5, 7]]
FAR_PAIRS = [(i, i ^ 1) for i in range(8)]
PAD_ROWS = 128
F32 = jnp.float32
BF16 = jnp.bfloat16


def spread(x, axis, groups=None):
    n = len(groups[0]) if groups else lax.axis_size(axis)
    copies = jnp.broadcast_to(x[None], (n,) + x.shape)
    return lax.all_to_all(copies, axis, 0, 0, tiled=True, axis_index_groups=groups)


def exchange(x, axis):
    n = lax.axis_size(axis)
    parts = x.reshape((n, x.shape[0] // n) + x.shape[1:])
    return lax.all_to_all(parts, axis, 0, 0, tiled=True)


def scatter_sum(x, axis):
    return jnp.sum(exchange(x, axis).astype(F32), axis=0)


def scatter_sum_gy(x):
    me = lax.axis_index("gy")
    ring, far = me >> 1, me & 1
    parts = x.reshape((4, 2, x.shape[0] // 8) + x.shape[1:])
    total = lax.dynamic_index_in_dim(parts, ring, 0, False).astype(F32)
    for k in (1, 2, 3):
        pairs = [(i, (i + 2 * k) % 8) for i in range(8)]
        sent = lax.dynamic_index_in_dim(parts, (ring + k) & 3, 0, False)
        total = total + lax.ppermute(sent, "gy", pairs).astype(F32)
    sent = lax.dynamic_index_in_dim(total, 1 - far, 0, False).astype(BF16)
    kept = lax.dynamic_index_in_dim(total, far, 0, False)
    return kept + lax.ppermute(sent, "gy", FAR_PAIRS).astype(F32)

def in_order(mine, other):
    first = (lax.axis_index("gy") & 1) == 0
    return jnp.where(first, jnp.stack([mine, other]), jnp.stack([other, mine]))


def all_sum_gz(x, later):
    both = lax.all_gather(x, "gz", axis=0, axis_index_groups=CORE_GROUPS)
    both = both.reshape((2, 2, x.shape[0] // 2) + x.shape[1:])
    half = lax.dynamic_index_in_dim(both, lax.axis_index("gz") & 1, 1, False)
    half = jnp.sum(half.astype(F32), axis=0).astype(BF16)
    rows = half.shape[0]
    run = lax.all_gather(half, "gz", axis=0, axis_index_groups=Y_GROUPS, tiled=True)
    run, later = lax.optimization_barrier((run, later))
    half = sum(run[i : i + rows].astype(F32) for i in range(0, 4 * rows, rows)).astype(BF16)
    return lax.all_gather(half, "gz", axis=0, axis_index_groups=CORE_GROUPS, tiled=True), later


def dot(a, b, dims):
    return lax.dot_general(a, b, (dims, ((), ())), preferred_element_type=F32)


def body(inputs, value_weight, probs, attended, out_weight, out_grad):
    tokens_all = probs.shape[1] * lax.axis_size("gz")
    grad_scale = 1.0 / math.sqrt(tokens_all)
    heads = probs.shape[0]
    width = heads * HEAD_DIM
    depth = value_weight.shape[0]

    side = lax.all_gather(jnp.concatenate([value_weight, attended]), "gx", axis=0)
    saved = side[:, depth:].reshape(-1, width)

    other = lax.ppermute(out_grad, "gy", FAR_PAIRS)
    quarter = lax.all_gather(out_weight, "gz", axis=0, axis_index_groups=Y_GROUPS)
    other, quarter, late = lax.optimization_barrier((other, quarter, inputs))
    grad_all = spread(in_order(out_grad, other), "gy", X_GROUPS).reshape(-1, out_grad.shape[1])
    quarter = quarter.reshape((-1,) + out_weight.shape)
    sibling = lax.ppermute(quarter, "gz", FAR_PAIRS)
    first = (lax.axis_index("gz") & 1) == 0
    halves = jnp.where(
        first, jnp.stack([quarter, sibling], 1), jnp.stack([sibling, quarter], 1)
    )
    out_all = halves.reshape(width, -1)

    head_partial = dot(grad_all, out_all, ((1,), (1,))).astype(BF16)
    head_parts = exchange(head_partial, "gx")
    other = lax.ppermute(late, "gy", FAR_PAIRS)
    out_terms = (dot(saved, grad_all, ((0,), (0,))) * grad_scale).astype(BF16)
    head_parts, out_terms, other = lax.optimization_barrier((head_parts, out_terms, other))
    head_rows = jnp.sum(head_parts.astype(F32), axis=0).astype(BF16)
    head_rows, other = lax.optimization_barrier((head_rows, other))
    mine = in_order(late, other).reshape(-1, inputs.shape[1])
    mine = jnp.pad(mine, ((0, PAD_ROWS), (0, 0)))
    weight_all = side[:, :depth].reshape(-1, width)
    head_all = spread(head_rows, "gx")
    input_all = lax.all_gather(mine, "gy", axis=0, axis_index_groups=X_GROUPS)
    head_all, weight_all = lax.optimization_barrier((head_all, weight_all))
    head_grad = head_all.reshape(-1, heads, HEAD_DIM)

    value_partial = jnp.einsum("hqk,qhd->khd", probs, head_grad, preferred_element_type=F32)
    value_partial = value_partial.reshape(-1, width).astype(BF16)
    value_grad, out_terms = all_sum_gz(value_partial, out_terms)
    grad_out_weight = lax.psum_scatter(out_terms, "gz", scatter_dimension=0, tiled=True)

    input_all = input_all[:, : 2 * inputs.shape[0]].reshape(-1, inputs.shape[1])
    value_terms = (dot(input_all, value_grad, ((0,), (0,))) * grad_scale).astype(BF16)
    input_partial = dot(value_grad, weight_all, ((1,), (1,))).astype(BF16)
    grad_value_weight = scatter_sum(value_terms, "gx")
    grad_inputs = scatter_sum_gy(input_partial)
    return grad_inputs.astype(BF16), grad_value_weight.astype(F32), grad_out_weight.astype(F32)


def solution(mesh):
    in_specs = (
        P(("gx", "gy"), "gz"),
        P(("gz", "gx"), "gy"),
        P("gy", "gz", "gx"),
        P(("gz", "gx"), "gy"),
        P(("gy", "gz"), "gx"),
        P(("gz", "gy"), "gx"),
    )
    out_specs = (P(("gx", "gy"), "gz"), P(("gz", "gx"), "gy"), P(("gy", "gz"), "gx"))
    return jax.shard_map(body, mesh=mesh, in_specs=in_specs, out_specs=out_specs, check_vma=False)
```

```python
import math

import jax
import jax.numpy as jnp
from jax import lax
from jax.sharding import PartitionSpec as P

HEAD_DIM = 128
Y_GROUPS = [[0, 2, 4, 6], [1, 3, 5, 7]]
CORE_GROUPS = [[0, 1], [2, 3], [4, 5], [6, 7]]
X_GROUPS = [[0, 2, 4, 6], [1, 3, 5, 7]]
FAR_PAIRS = [(i, i ^ 1) for i in range(8)]
PAD_ROWS = 128
F32 = jnp.float32
BF16 = jnp.bfloat16


def spread(x, axis, groups=None):
    n = len(groups[0]) if groups else lax.axis_size(axis)
    copies = jnp.broadcast_to(x[None], (n,) + x.shape)
    return lax.all_to_all(copies, axis, 0, 0, tiled=True, axis_index_groups=groups)


def exchange(x, axis):
    n = lax.axis_size(axis)
    parts = x.reshape((n, x.shape[0] // n) + x.shape[1:])
    return lax.all_to_all(parts, axis, 0, 0, tiled=True)


def scatter_sum(x, axis):
    return jnp.sum(exchange(x, axis).astype(F32), axis=0)


def scatter_sum_gy(x):
    me = lax.axis_index("gy")
    ring, far = me >> 1, me & 1
    parts = x.reshape((4, 2, x.shape[0] // 8) + x.shape[1:])
    total = lax.dynamic_index_in_dim(parts, ring, 0, False).astype(F32)
    for k in (1, 2, 3):
        pairs = [(i, (i + 2 * k) % 8) for i in range(8)]
        sent = lax.dynamic_index_in_dim(parts, (ring + k) & 3, 0, False)
        total = total + lax.ppermute(sent, "gy", pairs).astype(F32)
    sent = lax.dynamic_index_in_dim(total, 1 - far, 0, False).astype(BF16)
    kept = lax.dynamic_index_in_dim(total, far, 0, False)
    return kept + lax.ppermute(sent, "gy", FAR_PAIRS).astype(F32)

def in_order(mine, other):
    first = (lax.axis_index("gy") & 1) == 0
    return jnp.where(first, jnp.stack([mine, other]), jnp.stack([other, mine]))


def from_run(x, k):
    return lax.ppermute(x, "gz", [(i, i ^ (2 * k)) for i in range(8)])


def all_sum_gz(x, later):
    both = lax.all_gather(x, "gz", axis=0, axis_index_groups=CORE_GROUPS)
    both = both.reshape((2, 2, x.shape[0] // 2) + x.shape[1:])
    half = lax.dynamic_index_in_dim(both, lax.axis_index("gz") & 1, 1, False)
    half = jnp.sum(half.astype(F32), axis=0).astype(BF16)
    rows = half.shape[0]
    run = lax.all_gather(half, "gz", axis=0, axis_index_groups=Y_GROUPS, tiled=True)
    run, later = lax.optimization_barrier((run, later))
    half = sum(run[i : i + rows].astype(F32) for i in range(0, 4 * rows, rows)).astype(BF16)
    return lax.all_gather(half, "gz", axis=0, axis_index_groups=CORE_GROUPS, tiled=True), later


def dot(a, b, dims):
    return lax.dot_general(a, b, (dims, ((), ())), preferred_element_type=F32)


def body(inputs, value_weight, probs, attended, out_weight, out_grad):
    tokens_all = probs.shape[1] * lax.axis_size("gz")
    grad_scale = 1.0 / math.sqrt(tokens_all)
    heads = probs.shape[0]
    width = heads * HEAD_DIM
    depth = value_weight.shape[0]

    side = lax.all_gather(jnp.concatenate([value_weight, attended]), "gx", axis=0)

    other = lax.ppermute(out_grad, "gy", FAR_PAIRS)
    run = [out_weight] + [from_run(out_weight, k) for k in (1, 2, 3)]
    pair = in_order(out_grad, other).reshape(-1, out_grad.shape[1])
    grad_all = lax.all_gather(pair, "gy", axis=0, axis_index_groups=X_GROUPS, tiled=True)
    grad_all, *run, late = lax.optimization_barrier((grad_all, *run, inputs))
    place = lax.axis_index("gz") >> 1
    quarter = jnp.stack([lax.select_n(place ^ j, *run) for j in range(4)])
    sibling = lax.ppermute(quarter, "gz", FAR_PAIRS)
    first = (lax.axis_index("gz") & 1) == 0
    halves = jnp.where(
        first, jnp.stack([quarter, sibling], 1), jnp.stack([sibling, quarter], 1)
    )
    out_all = halves.reshape(width, -1)

    head_partial = dot(grad_all, out_all, ((1,), (1,))).astype(BF16)
    head_parts = exchange(head_partial, "gx")
    other = lax.ppermute(late, "gy", FAR_PAIRS)
    mine = in_order(late, other).reshape(-1, inputs.shape[1])
    mine = jnp.pad(mine, ((0, PAD_ROWS), (0, 0)))
    head_parts, mine = lax.optimization_barrier((head_parts, mine))
    input_all = lax.all_gather(mine, "gy", axis=0, axis_index_groups=X_GROUPS)
    head_rows = jnp.sum(head_parts.astype(F32), axis=0).astype(BF16)
    head_rows, grad_all = lax.optimization_barrier((head_rows, grad_all))
    weight_all = side[:, :depth].reshape(-1, width)
    saved = side[:, depth:].reshape(-1, width)
    out_terms = (dot(saved, grad_all, ((0,), (0,))) * grad_scale).astype(BF16)
    head_all = spread(head_rows, "gx")
    head_all, weight_all, out_terms = lax.optimization_barrier((head_all, weight_all, out_terms))
    head_grad = head_all.reshape(-1, heads, HEAD_DIM)

    value_partial = jnp.einsum("hqk,qhd->khd", probs, head_grad, preferred_element_type=F32)
    value_partial = value_partial.reshape(-1, width).astype(BF16)
    value_grad, out_terms = all_sum_gz(value_partial, out_terms)
    grad_out_weight = lax.psum_scatter(out_terms, "gz", scatter_dimension=0, tiled=True)

    input_all = input_all[:, : 2 * inputs.shape[0]].reshape(-1, inputs.shape[1])
    value_terms = (dot(input_all, value_grad, ((0,), (0,))) * grad_scale).astype(BF16)
    input_partial = dot(value_grad, weight_all, ((1,), (1,))).astype(BF16)
    grad_value_weight = scatter_sum(value_terms, "gx")
    grad_inputs = scatter_sum_gy(input_partial)
    return grad_inputs.astype(BF16), grad_value_weight.astype(F32), grad_out_weight.astype(F32)


def solution(mesh):
    in_specs = (
        P(("gx", "gy"), "gz"),
        P(("gz", "gx"), "gy"),
        P("gy", "gz", "gx"),
        P(("gz", "gx"), "gy"),
        P(("gy", "gz"), "gx"),
        P(("gz", "gy"), "gx"),
    )
    out_specs = (P(("gx", "gy"), "gz"), P(("gz", "gx"), "gy"), P(("gy", "gz"), "gx"))
    return jax.shard_map(body, mesh=mesh, in_specs=in_specs, out_specs=out_specs, check_vma=False)
```

```python
import math

import jax
import jax.numpy as jnp
from jax import lax
from jax.sharding import PartitionSpec as P

HEAD_DIM = 128
Y_GROUPS = [[0, 2, 4, 6], [1, 3, 5, 7]]
CORE_GROUPS = [[0, 1], [2, 3], [4, 5], [6, 7]]
X_GROUPS = [[0, 2, 4, 6], [1, 3, 5, 7]]
FAR_PAIRS = [(i, i ^ 1) for i in range(8)]
PAD_BLOCKS = 2
F32 = jnp.float32
BF16 = jnp.bfloat16


def spread(x, axis, groups=None):
    n = len(groups[0]) if groups else lax.axis_size(axis)
    copies = jnp.broadcast_to(x[None], (n,) + x.shape)
    return lax.all_to_all(copies, axis, 0, 0, tiled=True, axis_index_groups=groups)


def exchange(x, axis):
    n = lax.axis_size(axis)
    parts = x.reshape((n, x.shape[0] // n) + x.shape[1:])
    return lax.all_to_all(parts, axis, 0, 0, tiled=True)


def scatter_sum(x, axis):
    return jnp.sum(exchange(x, axis).astype(F32), axis=0)


def scatter_sum_gy(x):
    me = lax.axis_index("gy")
    ring, far = me >> 1, me & 1
    parts = x.reshape((4, 2, x.shape[0] // 8) + x.shape[1:])
    total = lax.dynamic_index_in_dim(parts, ring, 0, False).astype(F32)
    for k in (1, 2, 3):
        pairs = [(i, (i + 2 * k) % 8) for i in range(8)]
        sent = lax.dynamic_index_in_dim(parts, (ring + k) & 3, 0, False)
        total = total + lax.ppermute(sent, "gy", pairs).astype(F32)
    sent = lax.dynamic_index_in_dim(total, 1 - far, 0, False).astype(BF16)
    kept = lax.dynamic_index_in_dim(total, far, 0, False)
    return kept + lax.ppermute(sent, "gy", FAR_PAIRS).astype(F32)

def in_order(mine, other):
    first = (lax.axis_index("gy") & 1) == 0
    return jnp.where(first, jnp.stack([mine, other]), jnp.stack([other, mine]))


def from_run(x, k):
    return lax.ppermute(x, "gz", [(i, i ^ (2 * k)) for i in range(8)])


def all_sum_gz(x, later):
    both = lax.all_gather(x, "gz", axis=0, axis_index_groups=CORE_GROUPS)
    both = both.reshape((2, 2, x.shape[0] // 2) + x.shape[1:])
    half = lax.dynamic_index_in_dim(both, lax.axis_index("gz") & 1, 1, False)
    half = jnp.sum(half.astype(F32), axis=0).astype(BF16)
    rows = half.shape[0]
    run = lax.all_gather(half, "gz", axis=0, axis_index_groups=Y_GROUPS, tiled=True)
    run, later = lax.optimization_barrier((run, later))
    half = sum(run[i : i + rows].astype(F32) for i in range(0, 4 * rows, rows)).astype(BF16)
    return lax.all_gather(half, "gz", axis=0, axis_index_groups=CORE_GROUPS, tiled=True), later


def dot(a, b, dims):
    return lax.dot_general(a, b, (dims, ((), ())), preferred_element_type=F32)


def body(inputs, value_weight, probs, attended, out_weight, out_grad):
    tokens_all = probs.shape[1] * lax.axis_size("gz")
    grad_scale = 1.0 / math.sqrt(tokens_all)
    heads = probs.shape[0]
    width = heads * HEAD_DIM
    depth = value_weight.shape[0]

    side = lax.all_gather(jnp.concatenate([value_weight, attended]), "gx", axis=0)

    other = lax.ppermute(out_grad, "gy", FAR_PAIRS)
    run = [out_weight] + [from_run(out_weight, k) for k in (1, 2, 3)]
    pair = in_order(out_grad, other).reshape(-1, out_grad.shape[1])
    grad_all = lax.all_gather(pair, "gy", axis=0, axis_index_groups=X_GROUPS, tiled=True)
    grad_all, *run, late = lax.optimization_barrier((grad_all, *run, inputs))
    place = lax.axis_index("gz") >> 1
    quarter = jnp.stack([lax.select_n(place ^ j, *run) for j in range(4)])
    sibling = lax.ppermute(quarter, "gz", FAR_PAIRS)
    first = (lax.axis_index("gz") & 1) == 0
    halves = jnp.where(
        first, jnp.stack([quarter, sibling], 1), jnp.stack([sibling, quarter], 1)
    )
    out_all = halves.reshape(width, -1)

    head_partial = dot(grad_all, out_all, ((1,), (1,))).astype(BF16)
    head_parts = exchange(head_partial, "gx")
    other = lax.ppermute(late, "gy", FAR_PAIRS)
    mine = in_order(late, other).reshape(1, -1, inputs.shape[1])
    mine = jnp.pad(mine, ((0, PAD_BLOCKS), (0, 0), (0, 0)))
    head_parts, mine = lax.optimization_barrier((head_parts, mine))
    input_all = lax.all_gather(mine, "gy", axis=1, axis_index_groups=X_GROUPS, tiled=True)
    head_rows = jnp.sum(head_parts.astype(F32), axis=0).astype(BF16)
    head_rows, grad_all = lax.optimization_barrier((head_rows, grad_all))
    weight_all = side[:, :depth].reshape(-1, width)
    saved = side[:, depth:].reshape(-1, width)
    out_terms = (dot(saved, grad_all, ((0,), (0,))) * grad_scale).astype(BF16)
    head_all = spread(head_rows, "gx")
    head_all, weight_all, out_terms = lax.optimization_barrier((head_all, weight_all, out_terms))
    head_grad = head_all.reshape(-1, heads, HEAD_DIM)

    value_partial = jnp.einsum("hqk,qhd->khd", probs, head_grad, preferred_element_type=F32)
    value_partial = value_partial.reshape(-1, width).astype(BF16)
    value_grad, out_terms = all_sum_gz(value_partial, out_terms)
    grad_out_weight = lax.psum_scatter(out_terms, "gz", scatter_dimension=0, tiled=True)

    input_all = input_all[0]
    value_terms = (dot(input_all, value_grad, ((0,), (0,))) * grad_scale).astype(BF16)
    input_partial = dot(value_grad, weight_all, ((1,), (1,))).astype(BF16)
    grad_value_weight = scatter_sum(value_terms, "gx")
    grad_inputs = scatter_sum_gy(input_partial)
    return grad_inputs.astype(BF16), grad_value_weight.astype(F32), grad_out_weight.astype(F32)


def solution(mesh):
    in_specs = (
        P(("gx", "gy"), "gz"),
        P(("gz", "gx"), "gy"),
        P("gy", "gz", "gx"),
        P(("gz", "gx"), "gy"),
        P(("gy", "gz"), "gx"),
        P(("gz", "gy"), "gx"),
    )
    out_specs = (P(("gx", "gy"), "gz"), P(("gz", "gx"), "gy"), P(("gy", "gz"), "gx"))
    return jax.shard_map(body, mesh=mesh, in_specs=in_specs, out_specs=out_specs, check_vma=False)
```

```python
import math

import jax
import jax.numpy as jnp
from jax import lax
from jax.sharding import PartitionSpec as P

HEAD_DIM = 128
Y_GROUPS = [[0, 2, 4, 6], [1, 3, 5, 7]]
CORE_GROUPS = [[0, 1], [2, 3], [4, 5], [6, 7]]
X_GROUPS = [[0, 2, 4, 6], [1, 3, 5, 7]]
FAR_PAIRS = [(i, i ^ 1) for i in range(8)]
PAD_BLOCKS = 2
F32 = jnp.float32
BF16 = jnp.bfloat16


def spread(x, axis, groups=None):
    n = len(groups[0]) if groups else lax.axis_size(axis)
    copies = jnp.broadcast_to(x[None], (n,) + x.shape)
    return lax.all_to_all(copies, axis, 0, 0, tiled=True, axis_index_groups=groups)


def exchange(x, axis):
    n = lax.axis_size(axis)
    parts = x.reshape((n, x.shape[0] // n) + x.shape[1:])
    return lax.all_to_all(parts, axis, 0, 0, tiled=True)


def scatter_sum(x, axis):
    return jnp.sum(exchange(x, axis).astype(F32), axis=0)


def scatter_sum_gy(x, beside):
    me = lax.axis_index("gy")
    ring, far = me >> 1, me & 1
    parts = x.reshape((4, 2, x.shape[0] // 8) + x.shape[1:])
    total = lax.dynamic_index_in_dim(parts, ring, 0, False).astype(F32)
    for k in (1, 2, 3):
        pairs = [(i, (i + 2 * k) % 8) for i in range(8)]
        sent = lax.dynamic_index_in_dim(parts, (ring + k) & 3, 0, False)
        total = total + lax.ppermute(sent, "gy", pairs).astype(F32)
    sent = lax.dynamic_index_in_dim(total, 1 - far, 0, False).astype(BF16)
    kept = lax.dynamic_index_in_dim(total, far, 0, False)
    received, beside = lax.optimization_barrier((lax.ppermute(sent, "gy", FAR_PAIRS), beside))
    return kept + received.astype(F32), beside

def in_order(mine, other):
    first = (lax.axis_index("gy") & 1) == 0
    return jnp.where(first, jnp.stack([mine, other]), jnp.stack([other, mine]))


def from_run(x, k):
    return lax.ppermute(x, "gz", [(i, i ^ (2 * k)) for i in range(8)])


def all_sum_gz(x, later):
    both = lax.all_gather(x, "gz", axis=0, axis_index_groups=CORE_GROUPS)
    both = both.reshape((2, 2, x.shape[0] // 2) + x.shape[1:])
    half = lax.dynamic_index_in_dim(both, lax.axis_index("gz") & 1, 1, False)
    half = jnp.sum(half.astype(F32), axis=0).astype(BF16)
    rows = half.shape[0]
    run = lax.all_gather(half, "gz", axis=0, axis_index_groups=Y_GROUPS, tiled=True)
    run, later = lax.optimization_barrier((run, later))
    half = sum(run[i : i + rows].astype(F32) for i in range(0, 4 * rows, rows)).astype(BF16)
    return lax.all_gather(half, "gz", axis=0, axis_index_groups=CORE_GROUPS, tiled=True), later


def dot(a, b, dims):
    return lax.dot_general(a, b, (dims, ((), ())), preferred_element_type=F32)


def body(inputs, value_weight, probs, attended, out_weight, out_grad):
    tokens_all = probs.shape[1] * lax.axis_size("gz")
    grad_scale = 1.0 / math.sqrt(tokens_all)
    heads = probs.shape[0]
    width = heads * HEAD_DIM
    depth = value_weight.shape[0]

    side = lax.all_gather(jnp.concatenate([value_weight, attended]), "gx", axis=0)

    other = lax.ppermute(out_grad, "gy", FAR_PAIRS)
    run = [out_weight] + [from_run(out_weight, k) for k in (1, 2, 3)]
    pair = in_order(out_grad, other).reshape(-1, out_grad.shape[1])
    grad_all = lax.all_gather(pair, "gy", axis=0, axis_index_groups=X_GROUPS, tiled=True)
    grad_all, *run, late = lax.optimization_barrier((grad_all, *run, inputs))
    place = lax.axis_index("gz") >> 1
    quarter = jnp.stack([lax.select_n(place ^ j, *run) for j in range(4)])
    sibling = lax.ppermute(quarter, "gz", FAR_PAIRS)
    first = (lax.axis_index("gz") & 1) == 0
    halves = jnp.where(
        first, jnp.stack([quarter, sibling], 1), jnp.stack([sibling, quarter], 1)
    )
    out_all = halves.reshape(width, -1)

    head_partial = dot(grad_all, out_all, ((1,), (1,))).astype(BF16)
    head_parts = exchange(head_partial, "gx")
    other = lax.ppermute(late, "gy", FAR_PAIRS)
    mine = in_order(late, other).reshape(1, -1, inputs.shape[1])
    mine = jnp.pad(mine, ((0, PAD_BLOCKS), (0, 0), (0, 0)))
    head_parts, mine = lax.optimization_barrier((head_parts, mine))
    input_all = lax.all_gather(mine, "gy", axis=1, axis_index_groups=X_GROUPS, tiled=True)
    head_rows = jnp.sum(head_parts.astype(F32), axis=0).astype(BF16)
    head_rows, grad_all = lax.optimization_barrier((head_rows, grad_all))
    weight_all = side[:, :depth].reshape(-1, width)
    saved = side[:, depth:].reshape(-1, width)
    out_terms = (dot(saved, grad_all, ((0,), (0,))) * grad_scale).astype(BF16)
    head_all = spread(head_rows, "gx")
    head_all, weight_all, out_terms = lax.optimization_barrier((head_all, weight_all, out_terms))
    head_grad = head_all.reshape(-1, heads, HEAD_DIM)

    value_partial = jnp.einsum("hqk,qhd->khd", probs, head_grad, preferred_element_type=F32)
    value_partial = value_partial.reshape(-1, width).astype(BF16)
    value_grad, out_terms = all_sum_gz(value_partial, out_terms)
    grad_out_weight = lax.psum_scatter(out_terms, "gz", scatter_dimension=0, tiled=True)

    input_all = input_all[0]
    value_terms = (dot(input_all, value_grad, ((0,), (0,))) * grad_scale).astype(BF16)
    input_partial = dot(value_grad, weight_all, ((1,), (1,))).astype(BF16)
    grad_value_weight = scatter_sum(value_terms, "gx")
    grad_out_weight = grad_out_weight.astype(F32)
    grad_inputs, grad_out_weight = scatter_sum_gy(input_partial, grad_out_weight)
    return grad_inputs.astype(BF16), grad_value_weight.astype(F32), grad_out_weight


def solution(mesh):
    in_specs = (
        P(("gx", "gy"), "gz"),
        P(("gz", "gx"), "gy"),
        P("gy", "gz", "gx"),
        P(("gz", "gx"), "gy"),
        P(("gy", "gz"), "gx"),
        P(("gz", "gy"), "gx"),
    )
    out_specs = (P(("gx", "gy"), "gz"), P(("gz", "gx"), "gy"), P(("gy", "gz"), "gx"))
    return jax.shard_map(body, mesh=mesh, in_specs=in_specs, out_specs=out_specs, check_vma=False)
```
